128 devices in a mesh: rows: 32 (over z, y, core), layer: 4 (over x).
Axes of the slice: x: 4, y: 4, z: 4, core: 2. Of those that a mesh axis runs over, the one named last changes fastest.
Arguments:
- train_grads: bfloat16 [32768, 8, 4096], P('rows', 'layer'), may hold values from -6 to 6
- query_grads: bfloat16 [256, 8, 4096], P('rows', 'layer'), may hold values from -0.059814453 to 0.059814453
- basis_out: float32 [8, 64, 64], P('layer'), may hold values from -0.75 to 0.75
- basis_in: float32 [8, 64, 64], P('layer'), may hold values from -0.75 to 0.75
- eigenvalues: float32 [8, 64, 64], P('layer'), may hold values from 0.02 to 2
- train_ids: int32 [32768], P('rows'), may hold values from 0 to 32767, each once
- query_ids: int32 [256], P('layer'), may hold values from 0 to 32767
Outputs:
- scores: float32 [32768, 256], P('rows', 'layer')
The draws below stay inside these ranges and needn't reach their ends.
Inputs may be any that keep to these rules, and one draw needn't show every extreme that they name: `train_ids`: every id of the slab appears in exactly one train row.
All inputs are finite; a program needn't handle non-finite values.
Results may differ from the reference program's by a relative error of at most 0.0029.
Values may be sent and summed in bfloat16 or wider, within the bound.
A program may use at most 128 MiB of HBM per device.

```python
import math
import jax
import jax.numpy as jnp
from jax import lax

BASIS = 64
PROJ = 4096
LAYERS = 8
TRAIN = 32768
QUERIES = 256


def place_ends(entries, key, low, top_value):
    dims = entries.shape
    place = [jax.random.randint(jax.random.fold_in(key, axis), (), 0, dims[axis]) for axis in range(len(dims))]
    entries = entries.at[tuple(place)].set(low)
    longest = dims.index(max(dims))
    place[longest] = (place[longest] + 1) % dims[longest]
    return entries.at[tuple(place)].set(top_value)


def level_of(key, shape, split, low, high):
    factor_of = 1.0
    for position, shards_of in split:
        heights = jax.random.uniform(jax.random.fold_in(jax.random.fold_in(key, 6), position), (shards_of,), jnp.float32, low / len(split), high / len(split))
        factor_of = factor_of * jnp.repeat(jnp.exp(heights), shape[position] // shards_of).reshape((-1,) + (1,) * (len(shape) - 1 - position))
    return factor_of


def gaussian(key, shape, spread, reach, split=(), kind=jnp.bfloat16):
    values = jax.random.normal(key, shape, jnp.float32) * spread
    if len(split) > 0:
        values = level_of(key, shape, split, -0.22, 0.18) * values
    return jnp.clip(values, min=-reach, max=reach).astype(kind)


def setup_inputs(seed: int = 0) -> dict:
    seeds = jax.random.split(jax.random.key(seed), 8)
    return {
        "train_grads": gaussian(seeds[0], (TRAIN, LAYERS, PROJ), 1.0, 6.0, ((0, 32), (1, 4))),
        "query_grads": gaussian(seeds[1], (QUERIES, LAYERS, PROJ), 0.01, 0.059814453, ((0, 32), (1, 4))),
        "basis_out": gaussian(seeds[2], (LAYERS, BASIS, BASIS), BASIS ** -0.5, 0.75, ((0, 4),), jnp.float32),
        "basis_in": gaussian(seeds[3], (LAYERS, BASIS, BASIS), BASIS ** -0.5, 0.75, ((0, 4),), jnp.float32),
        "eigenvalues": jnp.clip(jnp.exp(math.log(2.0) - 4.6051702 * jax.random.uniform(seeds[4], (LAYERS, BASIS, BASIS), jnp.float32) ** level_of(seeds[4], (LAYERS, BASIS, BASIS), ((0, 4),), -0.2, 0.2)), 0.02, 2.0),
        "train_ids": jax.random.permutation(seeds[5], TRAIN).astype(jnp.int32),
        "query_ids": place_ends(jax.random.randint(seeds[6], (QUERIES,), 0, TRAIN), jax.random.fold_in(seeds[6], 1), 0, TRAIN - 1).astype(jnp.int32),
    }


DAMPING = 0.1


def precondition(query_grads, basis_out, basis_in, eigenvalues):
    count, layers, proj = query_grads.shape
    side = basis_out.shape[1]
    hp = lax.Precision.HIGHEST
    grads = query_grads.astype(jnp.float32).reshape(count, layers, side, side)
    rotated = jnp.einsum('lao,qlab->qlob', basis_out, grads, precision=hp)
    rotated = jnp.einsum('qlob,lbi->qloi', rotated, basis_in, precision=hp)
    scaled = rotated / (eigenvalues[None] + DAMPING)
    back = jnp.einsum('lao,qloi->qlai', basis_out, scaled, precision=hp)
    back = jnp.einsum('qlai,lbi->qlab', back, basis_in, precision=hp)
    return back.reshape(count, layers, proj).astype(jnp.bfloat16)


def reference(train_grads, query_grads, basis_out, basis_in, eigenvalues, train_ids, query_ids):
    prepared = precondition(query_grads, basis_out, basis_in, eigenvalues)
    flat_train = train_grads.reshape(train_grads.shape[0], -1)
    flat_query = prepared.reshape(prepared.shape[0], -1)
    raw = lax.dot_general(flat_train, flat_query, (((1,), (1,)), ((), ())), preferred_element_type=jnp.float32)
    same = train_ids[:, None] == query_ids[None, :]
    return jnp.where(same, jnp.float32(0.0), raw)
```

```python
import functools

import jax
import jax.numpy as jnp
from jax import lax
from jax.experimental import pallas as pl
from jax.experimental.pallas import tpu as pltpu
from jax.sharding import PartitionSpec as P

DAMPING = 0.1
MESH = pl.DeviceIdType.MESH
PAIRS = 4
WIDE = 4096 // PAIRS
HALF = WIDE // 2
CB = WIDE // 128
NT = (((1,), (1,)), ((), ()))
NN = (((1,), (0,)), ((), ()))
F32, BF16 = jnp.float32, jnp.bfloat16

OPS = (
    "Z1p", "Z1m", "Z2", "Z3A", "Z3B", "Z4B",
    "Y1A", "Y1B", "Y2B", "Y3Ap", "Y3Am", "Y4A", "Y3Bp", "Y3Bm", "Y4B",
    "DA", "DB",
)
OP = {name: place for place, name in enumerate(OPS)}


def split(value):
    high = value.astype(BF16)
    return high, (value - high.astype(F32)).astype(BF16)


def dot(a, b, dims=NN):
    return lax.dot_general(a, b, dims, preferred_element_type=F32)


def dot3(a, b, dims=NN):
    ah, al = split(a)
    bh, bl = split(b)
    return dot(ah, bh, dims) + (dot(al, bh, dims) + dot(ah, bl, dims))


def diagonal(block):
    wide = jnp.concatenate([block] * 4, axis=1)
    tall = jnp.concatenate([wide] * 4, axis=0)
    row = lax.broadcasted_iota(jnp.int32, (256, 256), 0) // 64
    col = lax.broadcasted_iota(jnp.int32, (256, 256), 1) // 64
    return jnp.where(row == col, tall, 0.0)


def kernel(
    train, query, basis_out, basis_in, eigenvalues, tids, qids, out,
    x, raw, flat, shaped, g, zacc, part, sb1, rb1, sb2, rb2,
    train_sem, raw_sem, send, recv, rs_send, rs_recv,
):
    rows, lay = lax.axis_index("rows"), lax.axis_index("layer")
    core = lax.rem(rows, 2)
    y = lax.rem(rows // 2, 4)
    z = rows // 8

    def at(dz, dy):
        return (lax.rem(z + dz + 4, 4) * 8 + lax.rem(y + dy + 4, 4) * 2 + core, lay)

    zp, zm, yp, ym = at(1, 0), at(-1, 0), at(0, 1), at(0, -1)
    sib = (rows + 1 - 2 * core, lay)
    lay1 = lay + 1 - 2 * lax.rem(lay, 2)
    x1, x3 = (rows, lay1), (rows, 3 - lay)
    lay2 = 3 - lay1
    iz_p, iz_m = lax.rem(z + 1, 4), lax.rem(z + 3, 4)

    barrier = pltpu.get_barrier_semaphore()
    for other in (sib, zp, zm, yp, ym, x1, x3):
        pl.semaphore_signal(barrier, inc=1, device_id=other, device_id_type=MESH)

    own_raw = pltpu.make_async_copy(query, raw.at[core], raw_sem.at[2])
    own_raw.start()
    def train_copy(cb):
        return pltpu.make_async_copy(train.at[:, cb], x.at[cb], train_sem.at[cb])

    for cb in range(32):
        train_copy(cb).start()

    bo, bi = basis_out[core], basis_in[core]
    left = diagonal(bo)
    left_t = diagonal(bo.T)
    right = diagonal(bi)
    scale = eigenvalues[core] + DAMPING
    scale = jnp.concatenate([jnp.concatenate([scale] * 4, axis=1)] * 4, axis=0)

    pl.semaphore_wait(barrier, 7)
    swap = pltpu.make_async_remote_copy(
        src_ref=query, dst_ref=raw.at[core], send_sem=raw_sem.at[0], recv_sem=raw_sem.at[1],
        device_id=sib, device_id_type=MESH,
    )
    swap.start()
    own_raw.wait()
    swap.wait()

    flat[...] = raw.reshape(1024, 128)[...].astype(F32)
    low = lax.broadcasted_iota(jnp.int32, (32, 128), 1) < 64
    for grp in range(4):
        for jh in range(2):
            q0 = 4 * grp + 2 * jh
            n0 = flat[pl.ds(q0 * 64 + core, 32, 2), :]
            n1 = flat[pl.ds(q0 * 64 + 64 + core, 32, 2), :]
            shaped[jh, pl.ds(grp * 64, 32, 2), :] = jnp.where(low, n0, pltpu.roll(n1, 64, 1))
            shaped[jh, pl.ds(grp * 64 + 1, 32, 2), :] = jnp.where(low, pltpu.roll(n0, 64, 1), n1)
    grads = jnp.concatenate([shaped[0], shaped[1]], axis=1).astype(BF16)
    lh, ll = split(left_t)
    rotated = dot3(dot(lh, grads) + dot(ll, grads), right)
    back = dot3(dot3(left, rotated / scale), right, NT)
    shaped[0] = back[:, :128]
    shaped[1] = back[:, 128:]
    for grp in range(4):
        for jh in range(2):
            q0 = 4 * grp + 2 * jh
            even = shaped[jh, pl.ds(grp * 64, 32, 2), :]
            odd = shaped[jh, pl.ds(grp * 64 + 1, 32, 2), :]
            flat[pl.ds(q0 * 32, 32), :] = jnp.where(low, even, pltpu.roll(odd, 64, 1))
            flat[pl.ds(q0 * 32 + 32, 32), :] = jnp.where(low, pltpu.roll(even, 64, 1), odd)
    for cb in range(32):
        g[core, 0, z, :, cb * 128:(cb + 1) * 128] = flat[pl.ds(cb, 16, 32), :].astype(BF16)

    every = slice(None)
    near, far = pl.ds(0, 2), pl.ds(2, 2)

    def copies(p):
        zc = pl.ds(pl.multiple_of(p * WIDE, WIDE), HALF)
        yc = pl.ds(pl.multiple_of(p * WIDE + HALF, HALF), HALF)
        both = pl.ds(pl.multiple_of(p * WIDE, WIDE), WIDE)
        odd = lax.rem(p, 2)
        way = 1 - 2 * odd
        zw, yw = at(way, 0), at(0, -way)
        behind = lax.rem(z - way + 4, 4)
        hop = 1 + 2 * odd
        table = {
            "Z1p": ((0, z, zc), (0, z, zc), zp),
            "Z1m": ((0, z, zc), (0, z, zc), zm),
            "Z2": ((0, behind, zc), (0, behind, zc), zw),
            "Z3A": ((0, every, zc), (1, every, zc), ym),
            "Z3B": ((0, every, zc), (3, every, zc), yp),
            "Z4B": ((hop, every, zc), (2, every, zc), yw),
            "Y1A": ((0, z, yc), (1, z, yc), ym),
            "Y1B": ((0, z, yc), (3, z, yc), yp),
            "Y2B": ((hop, z, yc), (2, z, yc), yw),
            "Y3Ap": ((near, z, yc), (near, z, yc), zp),
            "Y3Am": ((near, z, yc), (near, z, yc), zm),
            "Y4A": ((near, behind, yc), (near, behind, yc), zw),
            "Y3Bp": ((far, z, yc), (far, z, yc), zp),
            "Y3Bm": ((far, z, yc), (far, z, yc), zm),
            "Y4B": ((far, behind, yc), (far, behind, yc), zw),
            "DA": ((near, every, both), (near, every, both), sib),
            "DB": ((far, every, both), (far, every, both), sib),
        }

        def make(name):
            (d0, z0, c0), (d1, z1, c1), device = table[name]
            return pltpu.make_async_remote_copy(
                src_ref=g.at[core, d0, z0, every, c0], dst_ref=g.at[core, d1, z1, every, c1],
                send_sem=send.at[OP[name], p], recv_sem=recv.at[OP[name], p],
                device_id=device, device_id_type=MESH,
            )

        return make

    def go(p, *names):
        make = copies(p)
        for name in names:
            make(name).start()

    def got(p, *names):
        make = copies(p)
        for name in names:
            make(name).wait_recv()

    def stage1(p):
        go(p, "Z1p", "Z1m", "Y1A", "Y1B")

    def stage2(p):
        got(p, "Z1p", "Z1m")
        go(p, "Z2")
        got(p, "Y1A")
        go(p, "Y3Ap", "Y3Am")

    def stage3(p):
        got(p, "Z2")
        go(p, "Z3A", "Z3B")
        got(p, "Y3Ap", "Y3Am")
        go(p, "Y4A")
        got(p, "Y1B")
        go(p, "Y2B")

    def stage4(p):
        got(p, "Z3A", "Y4A")
        go(p, "DA")
        got(p, "Z3B")
        go(p, "Z4B")
        got(p, "Y2B")
        go(p, "Y3Bp", "Y3Bm")

    def stage5(p):
        got(p, "Y3Bp", "Y3Bm")
        go(p, "Y4B")

    def stage6(p):
        got(p, "Z4B", "Y4B")
        go(p, "DB")

    xr = x.reshape(32, 2048, 128)
    first = lax.rem(lax.broadcasted_iota(jnp.int32, (2048, 128), 0), 2) == 0

    def product(side, p):
        got(p, "DA" if side == 0 else "DB")
        if side == 0:
            for j in range(CB):
                train_copy(p * CB + j).wait()
        cols = pl.ds(pl.multiple_of(p * WIDE, WIDE), WIDE)
        weights = jnp.concatenate(
            [
                g[layer, 2 * side + dy, iz, :, cols]
                for layer in range(2)
                for iz in range(4)
                for dy in range(2)
            ],
            axis=0,
        )
        lhs = jnp.concatenate([xr[p * CB + j] for j in range(CB)], axis=1)
        both = dot(lhs, weights, NT)
        zacc[...] += jnp.where(first, both[:, :128], both[:, 128:])

    def reduce_copy(side, step, h):
        src, dst = ((sb1, rb1), (sb2, rb2))[step]
        return pltpu.make_async_remote_copy(
            src_ref=src.at[side, h], dst_ref=dst.at[side, h],
            send_sem=rs_send.at[side, step, h], recv_sem=rs_recv.at[side, step, h],
            device_id=(x1, x3)[step ^ h], device_id_type=MESH,
        )

    mates = (lay1, 3 - lay)

    def target(side, which, h):
        return part[side, pl.ds(pl.multiple_of(which * 32, 32), 32), h * 512:(h + 1) * 512]

    def scatter1(side):
        both = zacc[pl.ds(0, 1024, 2), :] + zacc[pl.ds(1, 1024, 2), :]
        part[side] = both.T
        for h in range(2):
            sb1[side, h, 0] = target(side, mates[h], h).astype(BF16)
            sb1[side, h, 1] = target(side, lay2, h).astype(BF16)
            reduce_copy(side, 0, h).start()

    def scatter2(side):
        for h in range(2):
            reduce_copy(side, 0, h).wait_recv()
            sb2[side, h] = (target(side, mates[1 - h], h) + rb1[side, h, 1].astype(F32)).astype(BF16)
            reduce_copy(side, 1, h).start()

    def finish(side):
        for h in range(2):
            reduce_copy(side, 1, h).wait_recv()
            cols = slice(h * 512, (h + 1) * 512)
            total = target(side, lay, h) + rb1[side, h, 0].astype(F32) + rb2[side, h].astype(F32)
            for dy in range(2):
                place = pl.ds(pl.multiple_of(lax.rem(y + 2 * side + dy, 4) * 16, 16), 16)
                same = qids[place, :] == tids[:, cols]
                out[place, cols] = jnp.where(same, 0.0, total[dy * 16:(dy + 1) * 16])
        for step in range(2):
            for h in range(2):
                reduce_copy(side, step, h).wait_send()

    def when(p, what):
        pl.when(jnp.logical_and(p >= 0, p < PAIRS))(functools.partial(what, p))

    zacc[...] = jnp.zeros_like(zacc)
    for p in range(PAIRS):
        stage1(p)

    @pl.loop(0, PAIRS + 4)
    def _(s):
        when(s, stage2)
        when(s - 1, stage3)
        when(s - 2, stage4)
        when(s - 3, functools.partial(product, 0))
        when(s - 3, stage5)
        when(s - 4, stage6)

    scatter1(0)
    zacc[...] = jnp.zeros_like(zacc)

    @pl.loop(0, PAIRS)
    def _(p):
        product(1, p)
        pl.when(p == 1)(functools.partial(scatter2, 0))
        pl.when(p == 2)(functools.partial(finish, 0))

    scatter1(1)
    scatter2(1)
    finish(1)

    @pl.loop(0, PAIRS)
    def _(p):
        make = copies(p)
        for name in OPS:
            make(name).wait_send()


def body(train_grads, query_grads, basis_out, basis_in, eigenvalues, train_ids, query_ids):
    train = train_grads.reshape(1024, 2, 32, 128).transpose(0, 2, 1, 3)
    query = query_grads.reshape(8, 2, 32, 128).transpose(0, 2, 1, 3)
    vmem = pl.BlockSpec(memory_space=pltpu.VMEM)
    hbm = pl.BlockSpec(memory_space=pl.ANY)
    dma = pltpu.SemaphoreType.DMA
    scores = pl.pallas_call(
        kernel,
        out_shape=jax.ShapeDtypeStruct((64, 1024), F32),
        in_specs=[hbm, hbm, vmem, vmem, vmem, vmem, vmem],
        out_specs=vmem,
        scratch_shapes=[
            pltpu.VMEM((32, 1024, 2, 128), BF16),
            pltpu.VMEM((2, 8, 32, 2, 128), BF16),
            pltpu.VMEM((1024, 128), F32),
            pltpu.VMEM((2, 256, 128), F32),
            pltpu.VMEM((2, 4, 4, 16, 4096), BF16),
            pltpu.VMEM((2048, 128), F32),
            pltpu.VMEM((2, 128, 1024), F32),
            pltpu.VMEM((2, 2, 2, 32, 512), BF16),
            pltpu.VMEM((2, 2, 2, 32, 512), BF16),
            pltpu.VMEM((2, 2, 32, 512), BF16),
            pltpu.VMEM((2, 2, 32, 512), BF16),
            dma((32,)),
            dma((3,)),
            dma((len(OPS), PAIRS)),
            dma((len(OPS), PAIRS)),
            dma((2, 2, 2)),
            dma((2, 2, 2)),
        ],
        compiler_params=pltpu.CompilerParams(
            collective_id=0, has_side_effects=True, vmem_limit_bytes=56 * 2**20
        ),
    )(
        train, query, basis_out, basis_in, eigenvalues,
        train_ids.reshape(1, -1), query_ids.reshape(-1, 1),
    )
    return scores.T


def solution(mesh):
    placed = (
        P("rows", "layer", None),
        P("rows", "layer", None),
        P("layer", None, None),
        P("layer", None, None),
        P("layer", None, None),
        P("rows"),
        P("layer"),
    )
    return jax.shard_map(
        body, mesh=mesh, in_specs=placed, out_specs=P("rows", "layer"), check_vma=False
    )
```

```python
import functools

import jax
import jax.numpy as jnp
from jax import lax
from jax.experimental import pallas as pl
from jax.experimental.pallas import tpu as pltpu
from jax.sharding import PartitionSpec as P

DAMPING = 0.1
MESH = pl.DeviceIdType.MESH
PARTS = 8
WIDE = 4096 // PARTS
CB = WIDE // 128
ROWS = 512
NT = (((1,), (1,)), ((), ()))
NN = (((1,), (0,)), ((), ()))
F32, BF16 = jnp.float32, jnp.bfloat16

OPS = ("S1p", "S1m", "S1d", "S2p", "S2m", "S3", "D0", "Dp", "Dm", "D2")
OP = {name: place for place, name in enumerate(OPS)}


def split(value):
    high = value.astype(BF16)
    return high, (value - high.astype(F32)).astype(BF16)


def dot(a, b, dims=NN):
    return lax.dot_general(a, b, dims, preferred_element_type=F32)


def dot3(a, b, dims=NN):
    ah, al = split(a)
    bh, bl = split(b)
    return dot(ah, bh, dims) + (dot(al, bh, dims) + dot(ah, bl, dims))


def square(grid):
    return jnp.concatenate([jnp.concatenate(line, axis=1) for line in grid], axis=0)


def diagonal(blocks):
    row = lax.broadcasted_iota(jnp.int32, (256, 256), 0) // 64
    col = lax.broadcasted_iota(jnp.int32, (256, 256), 1) // 64
    return jnp.where(row == col, square([[block] * 4 for block in blocks]), 0.0)


def kernel(
    train, query, basis_out, basis_in, eigenvalues, tids, qids, out,
    x, flat, shaped, whole, outbox, g, zacc, part, sb1, rb1, sb2, rb2,
    train_sem, swap_sem, send, recv, rs_send, rs_recv,
):
    rows, lay = lax.axis_index("rows"), lax.axis_index("layer")
    core = lax.rem(rows, 2)
    y = lax.rem(rows // 2, 4)
    z = rows // 8

    def at(dz, dy):
        return (lax.rem(z + dz + 4, 4) * 8 + lax.rem(y + dy + 4, 4) * 2 + core, lay)

    def first_axis(k):
        return at(k * (1 - core), k * core)

    def second_axis(k):
        return at(k * core, k * (1 - core))

    a = jnp.where(core == 0, z, y)
    b = jnp.where(core == 0, y, z)
    sib = (rows + 1 - 2 * core, lay)
    lay1 = lay + 1 - 2 * lax.rem(lay, 2)
    x1, x3 = (rows, lay1), (rows, 3 - lay)
    lay2 = 3 - lay1

    barrier = pltpu.get_barrier_semaphore()
    for other in (sib, at(1, 0), at(-1, 0), at(0, 1), at(0, -1), first_axis(2), x1, x3):
        pl.semaphore_signal(barrier, inc=1, device_id=other, device_id_type=MESH)

    def train_copy(cb):
        return pltpu.make_async_copy(train.at[:, cb], x.at[cb], train_sem.at[cb])

    for cb in range(32):
        train_copy(cb).start()

    flat[...] = query.reshape(512, 128)[...].astype(F32)
    low = lax.broadcasted_iota(jnp.int32, (32, 128), 1) < 64
    for layer in range(2):
        for grp in range(2):
            for jh in range(2):
                q0 = 4 * grp + 2 * jh
                n0 = flat[pl.ds(q0 * 64 + layer, 32, 2), :]
                n1 = flat[pl.ds(q0 * 64 + 64 + layer, 32, 2), :]
                shaped[layer, jh, pl.ds(grp * 64, 32, 2), :] = jnp.where(low, n0, pltpu.roll(n1, 64, 1))
                shaped[layer, jh, pl.ds(grp * 64 + 1, 32, 2), :] = jnp.where(low, pltpu.roll(n0, 64, 1), n1)
    grads = jnp.concatenate(
        [jnp.concatenate([shaped[layer, 0], shaped[layer, 1]], axis=1) for layer in range(2)], axis=0
    ).astype(BF16)
    bo = (basis_out[0], basis_out[1])
    left = diagonal((bo[0], bo[0], bo[1], bo[1]))
    left_t = diagonal((bo[0].T, bo[0].T, bo[1].T, bo[1].T))
    right = [diagonal((basis_in[layer],) * 4) for layer in range(2)]
    scale = square([[eigenvalues[layer] + DAMPING] * 4 for layer in (0, 0, 1, 1)])

    def by_right(value, dims):
        return jnp.concatenate(
            [dot3(value[layer * 128:(layer + 1) * 128], right[layer], dims) for layer in range(2)], axis=0
        )

    lh, ll = split(left_t)
    rotated = by_right(dot(lh, grads) + dot(ll, grads), NN)
    back = by_right(dot3(left, rotated / scale), NT)
    for layer in range(2):
        for jh in range(2):
            shaped[layer, jh] = back[layer * 128:(layer + 1) * 128, jh * 128:(jh + 1) * 128]

    def unshape(layer, place, start):
        for grp in range(2):
            for jh in range(2):
                q0 = 4 * grp + 2 * jh
                even = shaped[layer, jh, pl.ds(grp * 64, 32, 2), :]
                odd = shaped[layer, jh, pl.ds(grp * 64 + 1, 32, 2), :]
                first = pl.multiple_of(start + q0 * 32, 32)
                place[pl.ds(first, 32), :] = jnp.where(low, even, pltpu.roll(odd, 64, 1))
                place[pl.ds(first + 32, 32), :] = jnp.where(low, pltpu.roll(even, 64, 1), odd)

    unshape(1 - core, outbox, 0)
    unshape(core, whole, core * 256)
    zacc[...] = jnp.zeros_like(zacc)

    pl.semaphore_wait(barrier, 8)
    mine = pl.ds(pl.multiple_of(core * 256, 256), 256)
    swap = pltpu.make_async_remote_copy(
        src_ref=outbox, dst_ref=whole.at[mine], send_sem=swap_sem.at[0], recv_sem=swap_sem.at[1],
        device_id=sib, device_id_type=MESH,
    )
    swap.start()
    swap.wait()

    every = slice(None)

    ahead = [lax.rem(b + k, 4) for k in range(4)]
    devices = {
        "S1p": first_axis(1), "S1m": first_axis(-1), "S1d": first_axis(2),
        "S2p": second_axis(1), "S2m": second_axis(-1),
    }

    def copy(name, p, cols):
        odd = p % 2 if isinstance(p, int) else lax.rem(p, 2)

        def pick(even, other):
            if isinstance(odd, int):
                return other if odd else even
            return jnp.where(odd == 1, other, even)

        place, device = every, sib
        if name in ("S1p", "S1m", "S1d"):
            row, place, device = b, a, devices[name]
        elif name in ("S2p", "S2m"):
            row, device = b, devices[name]
        elif name == "S3":
            row = pick(ahead[3], ahead[1])
            device = (pick(devices["S2p"][0], devices["S2m"][0]), lay)
        else:
            row = ahead[{"D0": 0, "Dp": 1, "D2": 2, "Dm": 3}[name]]
        block = (core, row, place, every, cols)
        return pltpu.make_async_remote_copy(
            src_ref=g.at[block], dst_ref=g.at[block],
            send_sem=send.at[OP[name]], recv_sem=recv.at[OP[name], p],
            device_id=device, device_id_type=MESH,
        )

    def columns(p):
        start = p * WIDE if isinstance(p, int) else pl.multiple_of(p * WIDE, WIDE)
        return pl.ds(start, WIDE)

    def go(p, *names):
        for name in names:
            copy(name, p, columns(p)).start()

    def got(p, *names):
        for name in names:
            copy(name, p, columns(p)).wait_recv()

    def step2(p):
        got(p, "S1p", "S1m", "S1d")
        go(p, "S2p", "S2m", "D0")

    def step3(p):
        got(p, "S2p", "S2m")
        go(p, "S3", "Dp", "Dm")

    def step4(p):
        got(p, "S3")
        go(p, "D2")

    def ready(p):
        got(p, "D0", "Dp", "Dm", "D2")
        for j in range(CB):
            train_copy(p * CB + j).wait()

    xr = x.reshape(32, 2048, 128)
    even_row = lax.rem(lax.broadcasted_iota(jnp.int32, (ROWS, 128), 0), 2) == 0

    def weights(p):
        cols = pl.ds(pl.multiple_of(p * WIDE, WIDE), WIDE)
        blocks = [(0, iy, iz) for iz in range(4) for iy in range(4)] + [(1, iz, iy) for iz in range(4) for iy in range(4)]
        return jnp.concatenate([g[layer, i, j, :, cols] for layer, i, j in blocks], axis=0)

    def product(p, queries, r):
        span = slice(r * ROWS, (r + 1) * ROWS)
        lhs = jnp.concatenate([xr[p * CB + j, span, :] for j in range(CB)], axis=1)
        both = dot(lhs, queries, NT)
        for half in range(2):
            q = half * 128
            zacc[half, span] += jnp.where(even_row, both[:, q:q + 128], both[:, q + 256:q + 384])

    def products(p):
        ready(p)
        queries = weights(p)
        for r in range(2048 // ROWS):
            product(p, queries, r)

    def reduce_copy(step, r):
        src, dst = ((sb1, rb1), (sb2, rb2))[step]
        return pltpu.make_async_remote_copy(
            src_ref=src.at[r], dst_ref=dst.at[r],
            send_sem=rs_send.at[step, r], recv_sem=rs_recv.at[step, r],
            device_id=(x1, x3)[step ^ (r % 2)], device_id_type=MESH,
        )

    mates = (lay1, 3 - lay)

    def target(which, r):
        return part[pl.ds(pl.multiple_of(which * 64, 64), 64), r * 256:(r + 1) * 256]

    def scatter1(r):
        for half in range(2):
            both = zacc[half, pl.ds(r * ROWS, 256, 2), :] + zacc[half, pl.ds(r * ROWS + 1, 256, 2), :]
            part[half * 128:(half + 1) * 128, r * 256:(r + 1) * 256] = both.T
        sb1[r, 0] = target(mates[r % 2], r).astype(BF16)
        sb1[r, 1] = target(lay2, r).astype(BF16)
        reduce_copy(0, r).start()

    def scatter2(r):
        reduce_copy(0, r).wait_recv()
        sb2[r] = (target(mates[1 - r % 2], r) + rb1[r, 1].astype(F32)).astype(BF16)
        reduce_copy(1, r).start()

    def finish(r):
        reduce_copy(1, r).wait_recv()
        cols = slice(r * 256, (r + 1) * 256)
        total = target(lay, r) + rb1[r, 0].astype(F32) + rb2[r].astype(F32)
        out[:, cols] = jnp.where(ids == tids[:, cols], 0.0, total)

    def when(p, top, what):
        pl.when(jnp.logical_and(p >= 0, p < top))(functools.partial(what, p))

    for p in range(PARTS):
        for cb in range(p * CB, (p + 1) * CB):
            g[core, b, a, :, cb * 128:(cb + 1) * 128] = whole[pl.ds(cb, 16, 32), :].astype(BF16)
        go(p, "S1p", "S1m", "S1d")

    @pl.loop(0, PARTS + 8 - 1)
    def _(s):
        when(s, PARTS, step2)
        when(s - 3, PARTS, step3)
        when(s - 6, PARTS, step4)
        when(s - 8, PARTS - 1, products)

    place = lax.broadcasted_iota(jnp.int32, (64, 64), 0) == lax.broadcasted_iota(jnp.int32, (64, 64), 1)
    ids = jnp.sum(jnp.where(place, qids[...].astype(F32), 0.0), axis=1, keepdims=True).astype(jnp.int32)
    last = PARTS - 1
    ready(last)
    queries = weights(last)
    for r in range(4):
        product(last, queries, r)
        scatter1(r)
    for r in range(4):
        scatter2(r)
    for r in range(4):
        finish(r)

    for name in OPS:
        copy(name, 0, every).wait_send()

    for step in range(2):
        for r in range(4):
            reduce_copy(step, r).wait_send()


def body(train_grads, query_grads, basis_out, basis_in, eigenvalues, train_ids, query_ids):
    train = train_grads.reshape(1024, 2, 32, 128).transpose(0, 2, 1, 3)
    query = query_grads.reshape(8, 2, 32, 128).transpose(0, 2, 1, 3)
    vmem = pl.BlockSpec(memory_space=pltpu.VMEM)
    hbm = pl.BlockSpec(memory_space=pl.ANY)
    dma = pltpu.SemaphoreType.DMA
    scores = pl.pallas_call(
        kernel,
        out_shape=jax.ShapeDtypeStruct((64, 1024), F32),
        in_specs=[hbm, vmem, vmem, vmem, vmem, vmem, vmem],
        out_specs=vmem,
        scratch_shapes=[
            pltpu.VMEM((32, 1024, 2, 128), BF16),
            pltpu.VMEM((512, 128), F32),
            pltpu.VMEM((2, 2, 128, 128), F32),
            pltpu.VMEM((512, 128), F32),
            pltpu.VMEM((256, 128), F32),
            pltpu.VMEM((2, 4, 4, 16, 4096), BF16),
            pltpu.VMEM((2, 2048, 128), F32),
            pltpu.VMEM((256, 1024), F32),
            pltpu.VMEM((4, 2, 64, 256), BF16),
            pltpu.VMEM((4, 2, 64, 256), BF16),
            pltpu.VMEM((4, 64, 256), BF16),
            pltpu.VMEM((4, 64, 256), BF16),
            dma((32,)),
            dma((2,)),
            dma((len(OPS),)),
            dma((len(OPS), PARTS)),
            dma((2, 4)),
            dma((2, 4)),
        ],
        compiler_params=pltpu.CompilerParams(
            collective_id=0, has_side_effects=True, vmem_limit_bytes=56 * 2**20
        ),
    )(
        train, query, basis_out, basis_in, eigenvalues,
        train_ids.reshape(1, -1), query_ids.reshape(1, -1),
    )
    return scores.T


def solution(mesh):
    placed = (
        P("rows", "layer", None),
        P("rows", "layer", None),
        P("layer", None, None),
        P("layer", None, None),
        P("layer", None, None),
        P("rows"),
        P("layer"),
    )
    return jax.shard_map(
        body, mesh=mesh, in_specs=placed, out_specs=P("rows", "layer"), check_vma=False
    )
```

```python
import functools

import jax
import jax.numpy as jnp
from jax import lax
from jax.experimental import pallas as pl
from jax.experimental.pallas import tpu as pltpu
from jax.sharding import PartitionSpec as P

DAMPING = 0.1
MESH = pl.DeviceIdType.MESH
PARTS = 8
WIDE = 4096 // PARTS
CB = WIDE // 128
ROWS = 512
NT = (((1,), (1,)), ((), ()))
NN = (((1,), (0,)), ((), ()))
F32, BF16 = jnp.float32, jnp.bfloat16

OPS = ("S1p", "S1m", "S1d", "S2p", "S2m", "S3", "D0", "Dp", "Dm", "D2")
OP = {name: place for place, name in enumerate(OPS)}


def split(value):
    high = value.astype(BF16)
    return high, (value - high.astype(F32)).astype(BF16)


def dot(a, b, dims=NN):
    return lax.dot_general(a, b, dims, preferred_element_type=F32)


def dot3(a, b, dims=NN):
    ah, al = split(a)
    bh, bl = split(b)
    return dot(ah, bh, dims) + (dot(al, bh, dims) + dot(ah, bl, dims))


def square(grid):
    return jnp.concatenate([jnp.concatenate(line, axis=1) for line in grid], axis=0)


def diagonal(blocks):
    row = lax.broadcasted_iota(jnp.int32, (256, 256), 0) // 64
    col = lax.broadcasted_iota(jnp.int32, (256, 256), 1) // 64
    return jnp.where(row == col, square([[block] * 4 for block in blocks]), 0.0)


def kernel(
    train, query_in, basis_out_in, basis_in_in, eigenvalues_in, tids_in, qids_in, out,
    query, basis_out, basis_in, eigenvalues, tids, qids, x, flat, shaped, whole, outbox, g, zacc, part, sb1, rb1, sb2, rb2,
    load_sem, train_sem, swap_sem, send, recv, rs_send, rs_recv,
):
    rows, lay = lax.axis_index("rows"), lax.axis_index("layer")
    core = lax.rem(rows, 2)
    y = lax.rem(rows // 2, 4)
    z = rows // 8

    def at(dz, dy):
        return (lax.rem(z + dz + 4, 4) * 8 + lax.rem(y + dy + 4, 4) * 2 + core, lay)

    def first_axis(k):
        return at(k * (1 - core), k * core)

    def second_axis(k):
        return at(k * core, k * (1 - core))

    a = jnp.where(core == 0, z, y)
    b = jnp.where(core == 0, y, z)
    sib = (rows + 1 - 2 * core, lay)
    lay1 = lay + 1 - 2 * lax.rem(lay, 2)
    x1, x3 = (rows, lay1), (rows, 3 - lay)
    lay2 = 3 - lay1

    barrier = pltpu.get_barrier_semaphore()
    for other in (sib, at(1, 0), at(-1, 0), at(0, 1), at(0, -1), first_axis(2), x1, x3):
        pl.semaphore_signal(barrier, inc=1, device_id=other, device_id_type=MESH)

    loads = [
        pltpu.make_async_copy(src, dst, load_sem.at[place])
        for place, (src, dst) in enumerate((
            (query_in, query), (basis_out_in, basis_out), (basis_in_in, basis_in),
            (eigenvalues_in, eigenvalues), (tids_in, tids), (qids_in, qids),
        ))
    ]
    for load in loads:
        load.start()

    def train_copy(cb):
        return pltpu.make_async_copy(train.at[:, cb], x.at[cb], train_sem.at[cb])

    for cb in range(32):
        train_copy(cb).start()

    for load in loads:
        load.wait()
    flat[...] = query.reshape(512, 128)[...].astype(F32)
    low = lax.broadcasted_iota(jnp.int32, (32, 128), 1) < 64
    for layer in range(2):
        for grp in range(2):
            for jh in range(2):
                q0 = 4 * grp + 2 * jh
                n0 = flat[pl.ds(q0 * 64 + layer, 32, 2), :]
                n1 = flat[pl.ds(q0 * 64 + 64 + layer, 32, 2), :]
                shaped[layer, jh, pl.ds(grp * 64, 32, 2), :] = jnp.where(low, n0, pltpu.roll(n1, 64, 1))
                shaped[layer, jh, pl.ds(grp * 64 + 1, 32, 2), :] = jnp.where(low, pltpu.roll(n0, 64, 1), n1)
    grads = jnp.concatenate(
        [jnp.concatenate([shaped[layer, 0], shaped[layer, 1]], axis=1) for layer in range(2)], axis=0
    ).astype(BF16)
    bo = (basis_out[0], basis_out[1])
    left = diagonal((bo[0], bo[0], bo[1], bo[1]))
    left_t = diagonal((bo[0].T, bo[0].T, bo[1].T, bo[1].T))
    right = [diagonal((basis_in[layer],) * 4) for layer in range(2)]
    scale = square([[eigenvalues[layer] + DAMPING] * 4 for layer in (0, 0, 1, 1)])

    def by_right(value, dims):
        return jnp.concatenate(
            [dot3(value[layer * 128:(layer + 1) * 128], right[layer], dims) for layer in range(2)], axis=0
        )

    lh, ll = split(left_t)
    rotated = by_right(dot(lh, grads) + dot(ll, grads), NN)
    back = by_right(dot3(left, rotated / scale), NT)
    for layer in range(2):
        for jh in range(2):
            shaped[layer, jh] = back[layer * 128:(layer + 1) * 128, jh * 128:(jh + 1) * 128]

    def unshape(layer, place, start):
        for grp in range(2):
            for jh in range(2):
                q0 = 4 * grp + 2 * jh
                even = shaped[layer, jh, pl.ds(grp * 64, 32, 2), :]
                odd = shaped[layer, jh, pl.ds(grp * 64 + 1, 32, 2), :]
                first = pl.multiple_of(start + q0 * 32, 32)
                place[pl.ds(first, 32), :] = jnp.where(low, even, pltpu.roll(odd, 64, 1))
                place[pl.ds(first + 32, 32), :] = jnp.where(low, pltpu.roll(even, 64, 1), odd)

    unshape(1 - core, outbox, 0)
    unshape(core, whole, core * 256)
    zacc[...] = jnp.zeros_like(zacc)

    pl.semaphore_wait(barrier, 8)
    mine = pl.ds(pl.multiple_of(core * 256, 256), 256)
    swap = pltpu.make_async_remote_copy(
        src_ref=outbox, dst_ref=whole.at[mine], send_sem=swap_sem.at[0], recv_sem=swap_sem.at[1],
        device_id=sib, device_id_type=MESH,
    )
    swap.start()
    swap.wait()

    every = slice(None)

    ahead = [lax.rem(b + k, 4) for k in range(4)]
    devices = {
        "S1p": first_axis(1), "S1m": first_axis(-1), "S1d": first_axis(2),
        "S2p": second_axis(1), "S2m": second_axis(-1),
    }

    def copy(name, p, cols):
        odd = p % 2 if isinstance(p, int) else lax.rem(p, 2)

        def pick(even, other):
            if isinstance(odd, int):
                return other if odd else even
            return jnp.where(odd == 1, other, even)

        place, device = every, sib
        if name in ("S1p", "S1m", "S1d"):
            row, place, device = b, a, devices[name]
        elif name in ("S2p", "S2m"):
            row, device = b, devices[name]
        elif name == "S3":
            row = pick(ahead[3], ahead[1])
            device = (pick(devices["S2p"][0], devices["S2m"][0]), lay)
        else:
            row = ahead[{"D0": 0, "Dp": 1, "D2": 2, "Dm": 3}[name]]
        block = (core, row, place, every, cols)
        return pltpu.make_async_remote_copy(
            src_ref=g.at[block], dst_ref=g.at[block],
            send_sem=send.at[OP[name]], recv_sem=recv.at[OP[name], p],
            device_id=device, device_id_type=MESH,
        )

    def columns(p):
        start = p * WIDE if isinstance(p, int) else pl.multiple_of(p * WIDE, WIDE)
        return pl.ds(start, WIDE)

    def go(p, *names):
        for name in names:
            copy(name, p, columns(p)).start()

    def got(p, *names):
        for name in names:
            copy(name, p, columns(p)).wait_recv()

    def step2(p):
        got(p, "S1p", "S1m", "S1d")
        go(p, "S2p", "S2m", "D0")

    def step3(p):
        got(p, "S2p", "S2m")
        go(p, "S3", "Dp", "Dm")

    def step4(p):
        got(p, "S3")
        go(p, "D2")

    def ready(p):
        got(p, "D0", "Dp", "Dm", "D2")
        for j in range(CB):
            train_copy(p * CB + j).wait()

    xr = x.reshape(32, 2048, 128)
    even_row = lax.rem(lax.broadcasted_iota(jnp.int32, (ROWS, 128), 0), 2) == 0

    def weights(p):
        cols = pl.ds(pl.multiple_of(p * WIDE, WIDE), WIDE)
        blocks = [(0, iy, iz) for iz in range(4) for iy in range(4)] + [(1, iz, iy) for iz in range(4) for iy in range(4)]
        return jnp.concatenate([g[layer, i, j, :, cols] for layer, i, j in blocks], axis=0)

    def product(p, queries, r):
        span = slice(r * ROWS, (r + 1) * ROWS)
        lhs = jnp.concatenate([xr[p * CB + j, span, :] for j in range(CB)], axis=1)
        both = dot(lhs, queries, NT)
        for half in range(2):
            q = half * 128
            zacc[half, span] += jnp.where(even_row, both[:, q:q + 128], both[:, q + 256:q + 384])

    def products(p):
        ready(p)
        queries = weights(p)
        for r in range(2048 // ROWS):
            product(p, queries, r)

    def reduce_copy(step, r):
        src, dst = ((sb1, rb1), (sb2, rb2))[step]
        return pltpu.make_async_remote_copy(
            src_ref=src.at[r], dst_ref=dst.at[r],
            send_sem=rs_send.at[step, r], recv_sem=rs_recv.at[step, r],
            device_id=(x1, x3)[step ^ (r % 2)], device_id_type=MESH,
        )

    mates = (lay1, 3 - lay)

    def target(which, r):
        return part[pl.ds(pl.multiple_of(which * 64, 64), 64), r * 256:(r + 1) * 256]

    def scatter1(r):
        for half in range(2):
            both = zacc[half, pl.ds(r * ROWS, 256, 2), :] + zacc[half, pl.ds(r * ROWS + 1, 256, 2), :]
            part[half * 128:(half + 1) * 128, r * 256:(r + 1) * 256] = both.T
        sb1[r, 0] = target(mates[r % 2], r).astype(BF16)
        sb1[r, 1] = target(lay2, r).astype(BF16)
        reduce_copy(0, r).start()

    def scatter2(r):
        reduce_copy(0, r).wait_recv()
        sb2[r] = (target(mates[1 - r % 2], r) + rb1[r, 1].astype(F32)).astype(BF16)
        reduce_copy(1, r).start()

    def finish(r):
        reduce_copy(1, r).wait_recv()
        cols = slice(r * 256, (r + 1) * 256)
        total = target(lay, r) + rb1[r, 0].astype(F32) + rb2[r].astype(F32)
        out[:, cols] = jnp.where(ids == tids[:, cols], 0.0, total)

    def when(p, top, what):
        pl.when(jnp.logical_and(p >= 0, p < top))(functools.partial(what, p))

    for p in range(PARTS):
        for cb in range(p * CB, (p + 1) * CB):
            g[core, b, a, :, cb * 128:(cb + 1) * 128] = whole[pl.ds(cb, 16, 32), :].astype(BF16)
        go(p, "S1p", "S1m", "S1d")

    @pl.loop(0, PARTS + 7 - 1)
    def _(s):
        when(s - 7, PARTS - 1, products)
        when(s, PARTS, step2)
        when(s - 3, PARTS, step3)
        when(s - 6, PARTS, step4)

    place = lax.broadcasted_iota(jnp.int32, (64, 64), 0) == lax.broadcasted_iota(jnp.int32, (64, 64), 1)
    ids = jnp.sum(jnp.where(place, qids[...].astype(F32), 0.0), axis=1, keepdims=True).astype(jnp.int32)
    last = PARTS - 1
    ready(last)
    queries = weights(last)
    for r in range(4):
        product(last, queries, r)
        scatter1(r)
    scatter2(0)
    scatter2(1)
    scatter2(2)
    finish(0)
    scatter2(3)
    finish(1)
    finish(2)
    finish(3)

    for name in OPS:
        copy(name, 0, every).wait_send()

    for step in range(2):
        for r in range(4):
            reduce_copy(step, r).wait_send()


def body(train_grads, query_grads, basis_out, basis_in, eigenvalues, train_ids, query_ids):
    train = train_grads.reshape(1024, 2, 32, 128).transpose(0, 2, 1, 3)
    query = query_grads.reshape(8, 2, 32, 128).transpose(0, 2, 1, 3)
    vmem = pl.BlockSpec(memory_space=pltpu.VMEM)
    hbm = pl.BlockSpec(memory_space=pltpu.HBM)
    dma = pltpu.SemaphoreType.DMA
    scores = pl.pallas_call(
        kernel,
        out_shape=jax.ShapeDtypeStruct((64, 1024), F32),
        in_specs=[hbm] * 7,
        out_specs=vmem,
        scratch_shapes=[
            pltpu.VMEM((8, 32, 2, 128), BF16),
            pltpu.VMEM((2, 64, 64), F32),
            pltpu.VMEM((2, 64, 64), F32),
            pltpu.VMEM((2, 64, 64), F32),
            pltpu.VMEM((1, 1024), jnp.int32),
            pltpu.VMEM((1, 64), jnp.int32),
            pltpu.VMEM((32, 1024, 2, 128), BF16),
            pltpu.VMEM((512, 128), F32),
            pltpu.VMEM((2, 2, 128, 128), F32),
            pltpu.VMEM((512, 128), F32),
            pltpu.VMEM((256, 128), F32),
            pltpu.VMEM((2, 4, 4, 16, 4096), BF16),
            pltpu.VMEM((2, 2048, 128), F32),
            pltpu.VMEM((256, 1024), F32),
            pltpu.VMEM((4, 2, 64, 256), BF16),
            pltpu.VMEM((4, 2, 64, 256), BF16),
            pltpu.VMEM((4, 64, 256), BF16),
            pltpu.VMEM((4, 64, 256), BF16),
            dma((6,)),
            dma((32,)),
            dma((2,)),
            dma((len(OPS),)),
            dma((len(OPS), PARTS)),
            dma((2, 4)),
            dma((2, 4)),
        ],
        compiler_params=pltpu.CompilerParams(
            collective_id=0, has_side_effects=True, vmem_limit_bytes=50 * 2**20
        ),
    )(
        *(
            pltpu.with_memory_space_constraint(value, pltpu.HBM)
            for value in (
                train, query, basis_out, basis_in, eigenvalues,
                train_ids.reshape(1, -1), query_ids.reshape(1, -1),
            )
        )
    )
    return scores.T


def solution(mesh):
    placed = (
        P("rows", "layer", None),
        P("rows", "layer", None),
        P("layer", None, None),
        P("layer", None, None),
        P("layer", None, None),
        P("rows"),
        P("layer"),
    )
    return jax.shard_map(
        body, mesh=mesh, in_specs=placed, out_specs=P("rows", "layer"), check_vma=False
    )
```

```python
import functools

import jax
import jax.numpy as jnp
from jax import lax
from jax.experimental import pallas as pl
from jax.experimental.pallas import tpu as pltpu
from jax.sharding import PartitionSpec as P

DAMPING = 0.1
MESH = pl.DeviceIdType.MESH
PARTS = 8
WIDE = 4096 // PARTS
CB = WIDE // 128
ROWS = 512
NT = (((1,), (1,)), ((), ()))
NN = (((1,), (0,)), ((), ()))
F32, BF16 = jnp.float32, jnp.bfloat16

OPS = ("S1p", "S1m", "S1d", "S2p", "S2m", "S3", "D0", "Dp", "Dm", "D2")
OP = {name: place for place, name in enumerate(OPS)}


def split(value):
    high = value.astype(BF16)
    return high, (value - high.astype(F32)).astype(BF16)


def dot(a, b, dims=NN):
    return lax.dot_general(a, b, dims, preferred_element_type=F32)


def dot3(a, b, dims=NN):
    ah, al = split(a)
    bh, bl = split(b)
    return dot(ah, bh, dims) + (dot(al, bh, dims) + dot(ah, bl, dims))


def square(grid):
    return jnp.concatenate([jnp.concatenate(line, axis=1) for line in grid], axis=0)


def diagonal(blocks):
    row = lax.broadcasted_iota(jnp.int32, (256, 256), 0) // 64
    col = lax.broadcasted_iota(jnp.int32, (256, 256), 1) // 64
    return jnp.where(row == col, square([[block] * 4 for block in blocks]), 0.0)


def kernel(
    train, query_in, basis_out_in, basis_in_in, eigenvalues_in, tids_in, qids_in, out,
    query, basis_out, basis_in, eigenvalues, tids, qids, x, flat, shaped, whole, outbox, g, zacc, part, sb1, rb1, sb2, rb2,
    load_sem, train_sem, swap_sem, send, recv, rs_send, rs_recv,
):
    rows, lay = lax.axis_index("rows"), lax.axis_index("layer")
    core = lax.rem(rows, 2)
    y = lax.rem(rows // 2, 4)
    z = rows // 8

    def at(dz, dy):
        return (lax.rem(z + dz + 4, 4) * 8 + lax.rem(y + dy + 4, 4) * 2 + core, lay)

    def first_axis(k):
        return at(k * (1 - core), k * core)

    def second_axis(k):
        return at(k * core, k * (1 - core))

    a = jnp.where(core == 0, z, y)
    b = jnp.where(core == 0, y, z)
    sib = (rows + 1 - 2 * core, lay)
    lay1 = lay + 1 - 2 * lax.rem(lay, 2)
    x1, x3 = (rows, lay1), (rows, 3 - lay)
    lay2 = 3 - lay1

    barrier = pltpu.get_barrier_semaphore()
    for other in (sib, at(1, 0), at(-1, 0), at(0, 1), at(0, -1), first_axis(2), x1, x3):
        pl.semaphore_signal(barrier, inc=1, device_id=other, device_id_type=MESH)

    loads = [
        pltpu.make_async_copy(src, dst, load_sem.at[place])
        for place, (src, dst) in enumerate((
            (query_in, query), (basis_out_in, basis_out), (basis_in_in, basis_in),
            (eigenvalues_in, eigenvalues), (tids_in, tids), (qids_in, qids),
        ))
    ]
    for load in loads:
        load.start()

    def train_copy(cb):
        return pltpu.make_async_copy(train.at[:, cb], x.at[cb], train_sem.at[cb])

    for cb in range(32):
        train_copy(cb).start()

    for load in loads:
        load.wait()
    flat[...] = query.reshape(512, 128)[...].astype(F32)
    low = lax.broadcasted_iota(jnp.int32, (32, 128), 1) < 64
    for layer in range(2):
        for grp in range(2):
            for jh in range(2):
                q0 = 4 * grp + 2 * jh
                n0 = flat[pl.ds(q0 * 64 + layer, 32, 2), :]
                n1 = flat[pl.ds(q0 * 64 + 64 + layer, 32, 2), :]
                shaped[layer, jh, pl.ds(grp * 64, 32, 2), :] = jnp.where(low, n0, pltpu.roll(n1, 64, 1))
                shaped[layer, jh, pl.ds(grp * 64 + 1, 32, 2), :] = jnp.where(low, pltpu.roll(n0, 64, 1), n1)
    grads = jnp.concatenate(
        [jnp.concatenate([shaped[layer, 0], shaped[layer, 1]], axis=1) for layer in range(2)], axis=0
    ).astype(BF16)
    bo = (basis_out[0], basis_out[1])
    left = diagonal((bo[0], bo[0], bo[1], bo[1]))
    left_t = diagonal((bo[0].T, bo[0].T, bo[1].T, bo[1].T))
    right = [diagonal((basis_in[layer],) * 4) for layer in range(2)]
    scale = square([[eigenvalues[layer] + DAMPING] * 4 for layer in (0, 0, 1, 1)])

    def by_right(value, dims):
        return jnp.concatenate(
            [dot3(value[layer * 128:(layer + 1) * 128], right[layer], dims) for layer in range(2)], axis=0
        )

    lh, ll = split(left_t)
    rotated = by_right(dot(lh, grads) + dot(ll, grads), NN)
    back = by_right(dot3(left, rotated / scale), NT)
    for layer in range(2):
        for jh in range(2):
            shaped[layer, jh] = back[layer * 128:(layer + 1) * 128, jh * 128:(jh + 1) * 128]

    def unshape(layer, place, start):
        for grp in range(2):
            for jh in range(2):
                q0 = 4 * grp + 2 * jh
                even = shaped[layer, jh, pl.ds(grp * 64, 32, 2), :]
                odd = shaped[layer, jh, pl.ds(grp * 64 + 1, 32, 2), :]
                first = pl.multiple_of(start + q0 * 32, 32)
                place[pl.ds(first, 32), :] = jnp.where(low, even, pltpu.roll(odd, 64, 1))
                place[pl.ds(first + 32, 32), :] = jnp.where(low, pltpu.roll(even, 64, 1), odd)

    unshape(1 - core, outbox, 0)
    unshape(core, whole, core * 256)
    zacc[...] = jnp.zeros_like(zacc)

    pl.semaphore_wait(barrier, 8)
    mine = pl.ds(pl.multiple_of(core * 256, 256), 256)
    swap = pltpu.make_async_remote_copy(
        src_ref=outbox, dst_ref=whole.at[mine], send_sem=swap_sem.at[0], recv_sem=swap_sem.at[1],
        device_id=sib, device_id_type=MESH,
    )
    swap.start()
    swap.wait()

    every = slice(None)

    ahead = [lax.rem(b + k, 4) for k in range(4)]
    devices = {
        "S1p": first_axis(1), "S1m": first_axis(-1), "S1d": first_axis(2),
        "S2p": second_axis(1), "S2m": second_axis(-1),
    }

    def copy(name, p, cols):
        odd = p % 2 if isinstance(p, int) else lax.rem(p, 2)

        def pick(even, other):
            if isinstance(odd, int):
                return other if odd else even
            return jnp.where(odd == 1, other, even)

        place, device = every, sib
        if name in ("S1p", "S1m", "S1d"):
            row, place, device = b, a, devices[name]
        elif name in ("S2p", "S2m"):
            row, device = b, devices[name]
        elif name == "S3":
            row = pick(ahead[3], ahead[1])
            device = (pick(devices["S2p"][0], devices["S2m"][0]), lay)
        else:
            row = ahead[{"D0": 0, "Dp": 1, "D2": 2, "Dm": 3}[name]]
        block = (core, row, place, every, cols)
        return pltpu.make_async_remote_copy(
            src_ref=g.at[block], dst_ref=g.at[block],
            send_sem=send.at[OP[name]], recv_sem=recv.at[OP[name], p],
            device_id=device, device_id_type=MESH,
        )

    def columns(p):
        start = p * WIDE if isinstance(p, int) else pl.multiple_of(p * WIDE, WIDE)
        return pl.ds(start, WIDE)

    def go(p, *names):
        for name in names:
            copy(name, p, columns(p)).start()

    def got(p, *names):
        for name in names:
            copy(name, p, columns(p)).wait_recv()

    def step2(p):
        got(p, "S1p", "S1m", "S1d")
        go(p, "S2p", "S2m", "D0")

    def step3(p):
        got(p, "S2p", "S2m")
        go(p, "S3", "Dp", "Dm")

    def step4(p):
        got(p, "S3")
        go(p, "D2")

    def ready(p):
        got(p, "D0", "Dp", "Dm", "D2")
        for j in range(CB):
            train_copy(p * CB + j).wait()

    xr = x.reshape(32, 2048, 128)
    even_row = lax.rem(lax.broadcasted_iota(jnp.int32, (ROWS, 128), 0), 2) == 0

    def weights(p):
        cols = pl.ds(pl.multiple_of(p * WIDE, WIDE), WIDE)
        blocks = [(0, iy, iz) for iz in range(4) for iy in range(4)] + [(1, iz, iy) for iz in range(4) for iy in range(4)]
        return jnp.concatenate([g[layer, i, j, :, cols] for layer, i, j in blocks], axis=0)

    def product(p, queries, r):
        span = slice(r * ROWS, (r + 1) * ROWS)
        lhs = jnp.concatenate([xr[p * CB + j, span, :] for j in range(CB)], axis=1)
        both = dot(lhs, queries, NT)
        for half in range(2):
            q = half * 128
            zacc[half, span] += jnp.where(even_row, both[:, q:q + 128], both[:, q + 256:q + 384])

    def products(p):
        ready(p)
        queries = weights(p)
        for r in range(2048 // ROWS):
            product(p, queries, r)

    def reduce_copy(step, r):
        src, dst = ((sb1, rb1), (sb2, rb2))[step]
        return pltpu.make_async_remote_copy(
            src_ref=src.at[r], dst_ref=dst.at[r],
            send_sem=rs_send.at[step, r], recv_sem=rs_recv.at[step, r],
            device_id=(x1, x3)[step ^ (r % 2)], device_id_type=MESH,
        )

    mates = (lay1, 3 - lay)

    def target(which, r):
        return part[pl.ds(pl.multiple_of(which * 64, 64), 64), r * 256:(r + 1) * 256]

    def scatter1(r):
        for half in range(2):
            both = zacc[half, pl.ds(r * ROWS, 256, 2), :] + zacc[half, pl.ds(r * ROWS + 1, 256, 2), :]
            part[half * 128:(half + 1) * 128, r * 256:(r + 1) * 256] = both.T
        sb1[r, 0] = target(mates[r % 2], r).astype(BF16)
        sb1[r, 1] = target(lay2, r).astype(BF16)
        reduce_copy(0, r).start()

    def scatter2(r):
        reduce_copy(0, r).wait_recv()
        sb2[r] = (target(mates[1 - r % 2], r) + rb1[r, 1].astype(F32)).astype(BF16)
        reduce_copy(1, r).start()

    def finish(r):
        reduce_copy(1, r).wait_recv()
        cols = slice(r * 256, (r + 1) * 256)
        total = target(lay, r) + rb1[r, 0].astype(F32) + rb2[r].astype(F32)
        out[:, cols] = jnp.where(ids == tids[:, cols], 0.0, total)

    def when(p, top, what):
        pl.when(jnp.logical_and(p >= 0, p < top))(functools.partial(what, p))

    for p in range(PARTS):
        for cb in range(p * CB, (p + 1) * CB):
            g[core, b, a, :, cb * 128:(cb + 1) * 128] = whole[pl.ds(cb, 16, 32), :].astype(BF16)
        go(p, "S1p", "S1m", "S1d")

    @pl.loop(0, PARTS + 7 - 1)
    def _(s):
        when(s, PARTS, step2)
        when(s - 3, PARTS, step3)
        when(s - 6, PARTS, step4)
        when(s - 7, PARTS - 1, products)

    place = lax.broadcasted_iota(jnp.int32, (64, 64), 0) == lax.broadcasted_iota(jnp.int32, (64, 64), 1)
    ids = jnp.sum(jnp.where(place, qids[...].astype(F32), 0.0), axis=1, keepdims=True).astype(jnp.int32)
    last = PARTS - 1
    ready(last)
    queries = weights(last)
    for r in range(4):
        product(last, queries, r)
        scatter1(r)
    scatter2(0)
    scatter2(1)
    scatter2(2)
    finish(0)
    scatter2(3)
    finish(1)
    finish(2)
    finish(3)

    for name in OPS:
        copy(name, 0, every).wait_send()

    for step in range(2):
        for r in range(4):
            reduce_copy(step, r).wait_send()


def body(train_grads, query_grads, basis_out, basis_in, eigenvalues, train_ids, query_ids):
    train = train_grads.reshape(1024, 2, 32, 128).transpose(0, 2, 1, 3)
    query = query_grads.reshape(8, 2, 32, 128).transpose(0, 2, 1, 3)
    vmem = pl.BlockSpec(memory_space=pltpu.VMEM)
    hbm = pl.BlockSpec(memory_space=pltpu.HBM)
    dma = pltpu.SemaphoreType.DMA
    scores = pl.pallas_call(
        kernel,
        out_shape=jax.ShapeDtypeStruct((64, 1024), F32),
        in_specs=[hbm] * 7,
        out_specs=vmem,
        scratch_shapes=[
            pltpu.VMEM((8, 32, 2, 128), BF16),
            pltpu.VMEM((2, 64, 64), F32),
            pltpu.VMEM((2, 64, 64), F32),
            pltpu.VMEM((2, 64, 64), F32),
            pltpu.VMEM((1, 1024), jnp.int32),
            pltpu.VMEM((1, 64), jnp.int32),
            pltpu.VMEM((32, 1024, 2, 128), BF16),
            pltpu.VMEM((512, 128), F32),
            pltpu.VMEM((2, 2, 128, 128), F32),
            pltpu.VMEM((512, 128), F32),
            pltpu.VMEM((256, 128), F32),
            pltpu.VMEM((2, 4, 4, 16, 4096), BF16),
            pltpu.VMEM((2, 2048, 128), F32),
            pltpu.VMEM((256, 1024), F32),
            pltpu.VMEM((4, 2, 64, 256), BF16),
            pltpu.VMEM((4, 2, 64, 256), BF16),
            pltpu.VMEM((4, 64, 256), BF16),
            pltpu.VMEM((4, 64, 256), BF16),
            dma((6,)),
            dma((32,)),
            dma((2,)),
            dma((len(OPS),)),
            dma((len(OPS), PARTS)),
            dma((2, 4)),
            dma((2, 4)),
        ],
        compiler_params=pltpu.CompilerParams(
            collective_id=0, has_side_effects=True, vmem_limit_bytes=50 * 2**20
        ),
    )(
        *(
            pltpu.with_memory_space_constraint(value, pltpu.HBM)
            for value in (
                train, query, basis_out, basis_in, eigenvalues,
                train_ids.reshape(1, -1), query_ids.reshape(1, -1),
            )
        )
    )
    return scores.T


def solution(mesh):
    placed = (
        P("rows", "layer", None),
        P("rows", "layer", None),
        P("layer", None, None),
        P("layer", None, None),
        P("layer", None, None),
        P("rows"),
        P("layer"),
    )
    return jax.shard_map(
        body, mesh=mesh, in_specs=placed, out_specs=P("rows", "layer"), check_vma=False
    )
```

```python
import functools

import jax
import jax.numpy as jnp
from jax import lax
from jax.experimental import pallas as pl
from jax.experimental.pallas import tpu as pltpu
from jax.sharding import PartitionSpec as P

DAMPING = 0.1
MESH = pl.DeviceIdType.MESH
PARTS = 8
WIDE = 4096 // PARTS
CB = WIDE // 128
ROWS = 512
NT = (((1,), (1,)), ((), ()))
NN = (((1,), (0,)), ((), ()))
F32, BF16 = jnp.float32, jnp.bfloat16

OPS = ("S1p", "S1m", "S1d", "S2p", "S2m", "S3", "D0", "Dp", "Dm", "D2")
OP = {name: place for place, name in enumerate(OPS)}


def split(value):
    high = value.astype(BF16)
    return high, (value - high.astype(F32)).astype(BF16)


def dot(a, b, dims=NN):
    return lax.dot_general(a, b, dims, preferred_element_type=F32)


def dot3(a, b, dims=NN):
    ah, al = split(a)
    bh, bl = split(b)
    return dot(ah, bh, dims) + (dot(al, bh, dims) + dot(ah, bl, dims))


def square(grid):
    return jnp.concatenate([jnp.concatenate(line, axis=1) for line in grid], axis=0)


def diagonal(blocks):
    row = lax.broadcasted_iota(jnp.int32, (256, 256), 0) // 64
    col = lax.broadcasted_iota(jnp.int32, (256, 256), 1) // 64
    return jnp.where(row == col, square([[block] * 4 for block in blocks]), 0.0)


def kernel(
    train, query_in, basis_out_in, basis_in_in, eigenvalues_in, tids_in, qids_in, out,
    query, basis_out, basis_in, eigenvalues, tids, qids, x, flat, shaped, whole, outbox, g, zacc, part, sb1, rb1, sb2, rb2,
    load_sem, train_sem, swap_sem, send, recv, rs_send, rs_recv,
):
    rows, lay = lax.axis_index("rows"), lax.axis_index("layer")
    core = lax.rem(rows, 2)
    y = lax.rem(rows // 2, 4)
    z = rows // 8

    def at(dz, dy):
        return (lax.rem(z + dz + 4, 4) * 8 + lax.rem(y + dy + 4, 4) * 2 + core, lay)

    def first_axis(k):
        return at(k * (1 - core), k * core)

    def second_axis(k):
        return at(k * core, k * (1 - core))

    a = jnp.where(core == 0, z, y)
    b = jnp.where(core == 0, y, z)
    sib = (rows + 1 - 2 * core, lay)
    lay1 = lay + 1 - 2 * lax.rem(lay, 2)
    x1, x3 = (rows, lay1), (rows, 3 - lay)
    lay2 = 3 - lay1

    barrier = pltpu.get_barrier_semaphore()
    for other in (sib, at(1, 0), at(-1, 0), at(0, 1), at(0, -1), first_axis(2), x1, x3):
        pl.semaphore_signal(barrier, inc=1, device_id=other, device_id_type=MESH)

    loads = [
        pltpu.make_async_copy(src, dst, load_sem.at[place])
        for place, (src, dst) in enumerate((
            (query_in, query), (basis_out_in, basis_out), (basis_in_in, basis_in),
            (eigenvalues_in, eigenvalues), (tids_in, tids), (qids_in, qids),
        ))
    ]
    for load in loads:
        load.start()

    def train_copy(cb):
        return pltpu.make_async_copy(train.at[:, cb], x.at[cb], train_sem.at[cb])

    for load in loads:
        load.wait()
    for cb in range(32):
        train_copy(cb).start()

    flat[...] = query.reshape(512, 128)[...].astype(F32)
    low = lax.broadcasted_iota(jnp.int32, (32, 128), 1) < 64
    for layer in range(2):
        for grp in range(2):
            for jh in range(2):
                q0 = 4 * grp + 2 * jh
                n0 = flat[pl.ds(q0 * 64 + layer, 32, 2), :]
                n1 = flat[pl.ds(q0 * 64 + 64 + layer, 32, 2), :]
                shaped[layer, jh, pl.ds(grp * 64, 32, 2), :] = jnp.where(low, n0, pltpu.roll(n1, 64, 1))
                shaped[layer, jh, pl.ds(grp * 64 + 1, 32, 2), :] = jnp.where(low, pltpu.roll(n0, 64, 1), n1)
    grads = jnp.concatenate(
        [jnp.concatenate([shaped[layer, 0], shaped[layer, 1]], axis=1) for layer in range(2)], axis=0
    ).astype(BF16)
    bo = (basis_out[0], basis_out[1])
    left = diagonal((bo[0], bo[0], bo[1], bo[1]))
    left_t = diagonal((bo[0].T, bo[0].T, bo[1].T, bo[1].T))
    right = [diagonal((basis_in[layer],) * 4) for layer in range(2)]
    scale = square([[eigenvalues[layer] + DAMPING] * 4 for layer in (0, 0, 1, 1)])

    def by_right(value, dims):
        return jnp.concatenate(
            [dot3(value[layer * 128:(layer + 1) * 128], right[layer], dims) for layer in range(2)], axis=0
        )

    lh, ll = split(left_t)
    rotated = by_right(dot(lh, grads) + dot(ll, grads), NN)
    back = by_right(dot3(left, rotated / scale), NT)
    for layer in range(2):
        for jh in range(2):
            shaped[layer, jh] = back[layer * 128:(layer + 1) * 128, jh * 128:(jh + 1) * 128]

    def unshape(layer, place, start):
        for grp in range(2):
            for jh in range(2):
                q0 = 4 * grp + 2 * jh
                even = shaped[layer, jh, pl.ds(grp * 64, 32, 2), :]
                odd = shaped[layer, jh, pl.ds(grp * 64 + 1, 32, 2), :]
                first = pl.multiple_of(start + q0 * 32, 32)
                place[pl.ds(first, 32), :] = jnp.where(low, even, pltpu.roll(odd, 64, 1))
                place[pl.ds(first + 32, 32), :] = jnp.where(low, pltpu.roll(even, 64, 1), odd)

    unshape(1 - core, outbox, 0)
    unshape(core, whole, core * 256)
    zacc[...] = jnp.zeros_like(zacc)

    pl.semaphore_wait(barrier, 8)
    mine = pl.ds(pl.multiple_of(core * 256, 256), 256)
    swap = pltpu.make_async_remote_copy(
        src_ref=outbox, dst_ref=whole.at[mine], send_sem=swap_sem.at[0], recv_sem=swap_sem.at[1],
        device_id=sib, device_id_type=MESH,
    )
    swap.start()
    swap.wait()

    every = slice(None)

    ahead = [lax.rem(b + k, 4) for k in range(4)]
    devices = {
        "S1p": first_axis(1), "S1m": first_axis(-1), "S1d": first_axis(2),
        "S2p": second_axis(1), "S2m": second_axis(-1),
    }

    def copy(name, p, cols):
        odd = p % 2 if isinstance(p, int) else lax.rem(p, 2)

        def pick(even, other):
            if isinstance(odd, int):
                return other if odd else even
            return jnp.where(odd == 1, other, even)

        place, device = every, sib
        if name in ("S1p", "S1m", "S1d"):
            row, place, device = b, a, devices[name]
        elif name in ("S2p", "S2m"):
            row, device = b, devices[name]
        elif name == "S3":
            row = pick(ahead[3], ahead[1])
            device = (pick(devices["S2p"][0], devices["S2m"][0]), lay)
        else:
            row = ahead[{"D0": 0, "Dp": 1, "D2": 2, "Dm": 3}[name]]
        block = (core, row, place, every, cols)
        return pltpu.make_async_remote_copy(
            src_ref=g.at[block], dst_ref=g.at[block],
            send_sem=send.at[OP[name]], recv_sem=recv.at[OP[name], p],
            device_id=device, device_id_type=MESH,
        )

    def columns(p):
        start = p * WIDE if isinstance(p, int) else pl.multiple_of(p * WIDE, WIDE)
        return pl.ds(start, WIDE)

    def go(p, *names):
        for name in names:
            copy(name, p, columns(p)).start()

    def got(p, *names):
        for name in names:
            copy(name, p, columns(p)).wait_recv()

    def step2(p):
        got(p, "S1p", "S1m", "S1d")
        go(p, "S2p", "S2m", "D0")

    def step3(p):
        got(p, "S2p", "S2m")
        go(p, "S3", "Dp", "Dm")

    def step4(p):
        got(p, "S3")
        go(p, "D2")

    def ready(p):
        got(p, "D0", "Dp", "Dm", "D2")
        for j in range(CB):
            train_copy(p * CB + j).wait()

    xr = x.reshape(32, 2048, 128)
    even_row = lax.rem(lax.broadcasted_iota(jnp.int32, (ROWS, 128), 0), 2) == 0

    def weights(p):
        cols = pl.ds(pl.multiple_of(p * WIDE, WIDE), WIDE)
        blocks = [(0, iy, iz) for iz in range(4) for iy in range(4)] + [(1, iz, iy) for iz in range(4) for iy in range(4)]
        return jnp.concatenate([g[layer, i, j, :, cols] for layer, i, j in blocks], axis=0)

    def product(p, queries, r):
        span = slice(r * ROWS, (r + 1) * ROWS)
        lhs = jnp.concatenate([xr[p * CB + j, span, :] for j in range(CB)], axis=1)
        both = dot(lhs, queries, NT)
        for half in range(2):
            q = half * 128
            zacc[half, span] += jnp.where(even_row, both[:, q:q + 128], both[:, q + 256:q + 384])

    def products(p):
        ready(p)
        queries = weights(p)
        for r in range(2048 // ROWS):
            product(p, queries, r)

    def reduce_copy(step, r):
        src, dst = ((sb1, rb1), (sb2, rb2))[step]
        return pltpu.make_async_remote_copy(
            src_ref=src.at[r], dst_ref=dst.at[r],
            send_sem=rs_send.at[step, r], recv_sem=rs_recv.at[step, r],
            device_id=(x1, x3)[step ^ (r % 2)], device_id_type=MESH,
        )

    mates = (lay1, 3 - lay)

    def target(which, r):
        return part[pl.ds(pl.multiple_of(which * 64, 64), 64), r * 256:(r + 1) * 256]

    def scatter1(r):
        for half in range(2):
            both = zacc[half, pl.ds(r * ROWS, 256, 2), :] + zacc[half, pl.ds(r * ROWS + 1, 256, 2), :]
            part[half * 128:(half + 1) * 128, r * 256:(r + 1) * 256] = both.T
        sb1[r, 0] = target(mates[r % 2], r).astype(BF16)
        sb1[r, 1] = target(lay2, r).astype(BF16)
        reduce_copy(0, r).start()

    def scatter2(r):
        reduce_copy(0, r).wait_recv()
        sb2[r] = (target(mates[1 - r % 2], r) + rb1[r, 1].astype(F32)).astype(BF16)
        reduce_copy(1, r).start()

    def finish(r):
        reduce_copy(1, r).wait_recv()
        cols = slice(r * 256, (r + 1) * 256)
        total = target(lay, r) + rb1[r, 0].astype(F32) + rb2[r].astype(F32)
        out[:, cols] = jnp.where(ids == tids[:, cols], 0.0, total)

    def when(p, top, what):
        pl.when(jnp.logical_and(p >= 0, p < top))(functools.partial(what, p))

    for p in range(PARTS):
        for cb in range(p * CB, (p + 1) * CB):
            g[core, b, a, :, cb * 128:(cb + 1) * 128] = whole[pl.ds(cb, 16, 32), :].astype(BF16)
        go(p, "S1p", "S1m", "S1d")

    @pl.loop(0, PARTS + 7 - 1)
    def _(s):
        when(s, PARTS, step2)
        when(s - 3, PARTS, step3)
        when(s - 6, PARTS, step4)
        when(s - 7, PARTS - 1, products)

    place = lax.broadcasted_iota(jnp.int32, (64, 64), 0) == lax.broadcasted_iota(jnp.int32, (64, 64), 1)
    ids = jnp.sum(jnp.where(place, qids[...].astype(F32), 0.0), axis=1, keepdims=True).astype(jnp.int32)
    last = PARTS - 1
    ready(last)
    queries = weights(last)
    for r in range(4):
        product(last, queries, r)
        scatter1(r)
    for r in range(4):
        scatter2(r)
    for r in range(4):
        finish(r)

    for name in OPS:
        copy(name, 0, every).wait_send()

    for step in range(2):
        for r in range(4):
            reduce_copy(step, r).wait_send()


def body(train_grads, query_grads, basis_out, basis_in, eigenvalues, train_ids, query_ids):
    train = train_grads.reshape(1024, 2, 32, 128).transpose(0, 2, 1, 3)
    query = query_grads.reshape(8, 2, 32, 128).transpose(0, 2, 1, 3)
    vmem = pl.BlockSpec(memory_space=pltpu.VMEM)
    hbm = pl.BlockSpec(memory_space=pltpu.HBM)
    dma = pltpu.SemaphoreType.DMA
    scores = pl.pallas_call(
        kernel,
        out_shape=jax.ShapeDtypeStruct((64, 1024), F32),
        in_specs=[hbm] * 7,
        out_specs=vmem,
        scratch_shapes=[
            pltpu.VMEM((8, 32, 2, 128), BF16),
            pltpu.VMEM((2, 64, 64), F32),
            pltpu.VMEM((2, 64, 64), F32),
            pltpu.VMEM((2, 64, 64), F32),
            pltpu.VMEM((1, 1024), jnp.int32),
            pltpu.VMEM((1, 64), jnp.int32),
            pltpu.VMEM((32, 1024, 2, 128), BF16),
            pltpu.VMEM((512, 128), F32),
            pltpu.VMEM((2, 2, 128, 128), F32),
            pltpu.VMEM((512, 128), F32),
            pltpu.VMEM((256, 128), F32),
            pltpu.VMEM((2, 4, 4, 16, 4096), BF16),
            pltpu.VMEM((2, 2048, 128), F32),
            pltpu.VMEM((256, 1024), F32),
            pltpu.VMEM((4, 2, 64, 256), BF16),
            pltpu.VMEM((4, 2, 64, 256), BF16),
            pltpu.VMEM((4, 64, 256), BF16),
            pltpu.VMEM((4, 64, 256), BF16),
            dma((6,)),
            dma((32,)),
            dma((2,)),
            dma((len(OPS),)),
            dma((len(OPS), PARTS)),
            dma((2, 4)),
            dma((2, 4)),
        ],
        compiler_params=pltpu.CompilerParams(
            collective_id=0, has_side_effects=True, vmem_limit_bytes=50 * 2**20
        ),
    )(
        *(
            pltpu.with_memory_space_constraint(value, pltpu.HBM)
            for value in (
                train, query, basis_out, basis_in, eigenvalues,
                train_ids.reshape(1, -1), query_ids.reshape(1, -1),
            )
        )
    )
    return scores.T


def solution(mesh):
    placed = (
        P("rows", "layer", None),
        P("rows", "layer", None),
        P("layer", None, None),
        P("layer", None, None),
        P("layer", None, None),
        P("rows"),
        P("layer"),
    )
    return jax.shard_map(
        body, mesh=mesh, in_specs=placed, out_specs=P("rows", "layer"), check_vma=False
    )
```

```python
import functools

import jax
import jax.numpy as jnp
from jax import lax
from jax.experimental import pallas as pl
from jax.experimental.pallas import tpu as pltpu
from jax.sharding import PartitionSpec as P

DAMPING = 0.1
MESH = pl.DeviceIdType.MESH
PARTS = 8
WIDE = 4096 // PARTS
CB = WIDE // 128
ROWS = 512
NT = (((1,), (1,)), ((), ()))
NN = (((1,), (0,)), ((), ()))
F32, BF16 = jnp.float32, jnp.bfloat16

OPS = ("S1p", "S1m", "S1d", "S2p", "S2m", "S3", "D0", "Dp", "Dm", "D2")
OP = {name: place for place, name in enumerate(OPS)}


def split(value):
    high = value.astype(BF16)
    return high, (value - high.astype(F32)).astype(BF16)


def dot(a, b, dims=NN):
    return lax.dot_general(a, b, dims, preferred_element_type=F32)


def dot3(a, b, dims=NN):
    ah, al = split(a)
    bh, bl = split(b)
    return dot(ah, bh, dims) + (dot(al, bh, dims) + dot(ah, bl, dims))


def square(grid):
    return jnp.concatenate([jnp.concatenate(line, axis=1) for line in grid], axis=0)


def diagonal(blocks):
    row = lax.broadcasted_iota(jnp.int32, (256, 256), 0) // 64
    col = lax.broadcasted_iota(jnp.int32, (256, 256), 1) // 64
    return jnp.where(row == col, square([[block] * 4 for block in blocks]), 0.0)


def kernel(
    train, query_in, basis_out_in, basis_in_in, eigenvalues_in, tids_in, qids_in, out,
    query, basis_out, basis_in, eigenvalues, tids, qids, x, flat, shaped, whole, outbox, g, zacc, part, sb1, rb1, sb2, rb2,
    load_sem, train_sem, swap_sem, send, recv, rs_send, rs_recv,
):
    rows, lay = lax.axis_index("rows"), lax.axis_index("layer")
    core = lax.rem(rows, 2)
    y = lax.rem(rows // 2, 4)
    z = rows // 8

    def at(dz, dy):
        return (lax.rem(z + dz + 4, 4) * 8 + lax.rem(y + dy + 4, 4) * 2 + core, lay)

    def first_axis(k):
        return at(k * (1 - core), k * core)

    def second_axis(k):
        return at(k * core, k * (1 - core))

    a = jnp.where(core == 0, z, y)
    b = jnp.where(core == 0, y, z)
    sib = (rows + 1 - 2 * core, lay)
    lay1 = lay + 1 - 2 * lax.rem(lay, 2)
    x1, x3 = (rows, lay1), (rows, 3 - lay)
    lay2 = 3 - lay1

    barrier = pltpu.get_barrier_semaphore()
    for other in (sib, at(1, 0), at(-1, 0), at(0, 1), at(0, -1), first_axis(2), x1, x3):
        pl.semaphore_signal(barrier, inc=1, device_id=other, device_id_type=MESH)

    loads = [
        pltpu.make_async_copy(src, dst, load_sem.at[place])
        for place, (src, dst) in enumerate((
            (query_in, query), (basis_out_in, basis_out), (basis_in_in, basis_in),
            (eigenvalues_in, eigenvalues), (tids_in, tids), (qids_in, qids),
        ))
    ]
    for load in loads:
        load.start()

    def train_copy(cb):
        return pltpu.make_async_copy(train.at[:, cb], x.at[cb], train_sem.at[cb])

    for load in loads:
        load.wait()
    for cb in range(32):
        train_copy(cb).start()

    flat[...] = query.reshape(512, 128)[...].astype(F32)
    low = lax.broadcasted_iota(jnp.int32, (32, 128), 1) < 64
    for layer in range(2):
        for grp in range(2):
            for jh in range(2):
                q0 = 4 * grp + 2 * jh
                n0 = flat[pl.ds(q0 * 64 + layer, 32, 2), :]
                n1 = flat[pl.ds(q0 * 64 + 64 + layer, 32, 2), :]
                shaped[layer, jh, pl.ds(grp * 64, 32, 2), :] = jnp.where(low, n0, pltpu.roll(n1, 64, 1))
                shaped[layer, jh, pl.ds(grp * 64 + 1, 32, 2), :] = jnp.where(low, pltpu.roll(n0, 64, 1), n1)
    grads = jnp.concatenate(
        [jnp.concatenate([shaped[layer, 0], shaped[layer, 1]], axis=1) for layer in range(2)], axis=0
    ).astype(BF16)
    bo = (basis_out[0], basis_out[1])
    left = diagonal((bo[0], bo[0], bo[1], bo[1]))
    left_t = diagonal((bo[0].T, bo[0].T, bo[1].T, bo[1].T))
    right = [diagonal((basis_in[layer],) * 4) for layer in range(2)]
    scale = square([[eigenvalues[layer] + DAMPING] * 4 for layer in (0, 0, 1, 1)])

    def by_right(value, dims):
        return jnp.concatenate(
            [dot3(value[layer * 128:(layer + 1) * 128], right[layer], dims) for layer in range(2)], axis=0
        )

    lh, ll = split(left_t)
    rotated = by_right(dot(lh, grads) + dot(ll, grads), NN)
    back = by_right(dot3(left, rotated / scale), NT)
    for layer in range(2):
        for jh in range(2):
            shaped[layer, jh] = back[layer * 128:(layer + 1) * 128, jh * 128:(jh + 1) * 128]

    def unshape(layer, place, start):
        for grp in range(2):
            for jh in range(2):
                q0 = 4 * grp + 2 * jh
                even = shaped[layer, jh, pl.ds(grp * 64, 32, 2), :]
                odd = shaped[layer, jh, pl.ds(grp * 64 + 1, 32, 2), :]
                first = pl.multiple_of(start + q0 * 32, 32)
                place[pl.ds(first, 32), :] = jnp.where(low, even, pltpu.roll(odd, 64, 1))
                place[pl.ds(first + 32, 32), :] = jnp.where(low, pltpu.roll(even, 64, 1), odd)

    unshape(1 - core, outbox, 0)
    unshape(core, whole, core * 256)
    zacc[...] = jnp.zeros_like(zacc)

    pl.semaphore_wait(barrier, 8)
    mine = pl.ds(pl.multiple_of(core * 256, 256), 256)
    swap = pltpu.make_async_remote_copy(
        src_ref=outbox, dst_ref=whole.at[mine], send_sem=swap_sem.at[0], recv_sem=swap_sem.at[1],
        device_id=sib, device_id_type=MESH,
    )
    swap.start()
    swap.wait()

    every = slice(None)

    ahead = [lax.rem(b + k, 4) for k in range(4)]
    devices = {
        "S1p": first_axis(1), "S1m": first_axis(-1), "S1d": first_axis(2),
        "S2p": second_axis(1), "S2m": second_axis(-1),
    }

    def copy(name, p, cols):
        odd = p % 2 if isinstance(p, int) else lax.rem(p, 2)

        def pick(even, other):
            if isinstance(odd, int):
                return other if odd else even
            return jnp.where(odd == 1, other, even)

        place, device = every, sib
        if name in ("S1p", "S1m", "S1d"):
            row, place, device = b, a, devices[name]
        elif name in ("S2p", "S2m"):
            row, device = b, devices[name]
        elif name == "S3":
            row = pick(ahead[3], ahead[1])
            device = (pick(devices["S2p"][0], devices["S2m"][0]), lay)
        else:
            row = ahead[{"D0": 0, "Dp": 1, "D2": 2, "Dm": 3}[name]]
        block = (core, row, place, every, cols)
        return pltpu.make_async_remote_copy(
            src_ref=g.at[block], dst_ref=g.at[block],
            send_sem=send.at[OP[name]], recv_sem=recv.at[OP[name], p],
            device_id=device, device_id_type=MESH,
        )

    def columns(p):
        start = p * WIDE if isinstance(p, int) else pl.multiple_of(p * WIDE, WIDE)
        return pl.ds(start, WIDE)

    def go(p, *names):
        for name in names:
            copy(name, p, columns(p)).start()

    def got(p, *names):
        for name in names:
            copy(name, p, columns(p)).wait_recv()

    def step2(p):
        got(p, "S1p", "S1m", "S1d")
        go(p, "S2p", "S2m", "D0")

    def step3(p):
        got(p, "S2p", "S2m")
        go(p, "S3", "Dp", "Dm")

    def step4(p):
        got(p, "S3")
        go(p, "D2")

    def ready(p):
        got(p, "D0", "Dp", "Dm", "D2")
        for j in range(CB):
            train_copy(p * CB + j).wait()

    xr = x.reshape(32, 2048, 128)
    even_row = lax.rem(lax.broadcasted_iota(jnp.int32, (ROWS, 128), 0), 2) == 0

    def weights(p):
        cols = pl.ds(pl.multiple_of(p * WIDE, WIDE), WIDE)
        blocks = [(0, iy, iz) for iz in range(4) for iy in range(4)] + [(1, iz, iy) for iz in range(4) for iy in range(4)]
        return jnp.concatenate([g[layer, i, j, :, cols] for layer, i, j in blocks], axis=0)

    def product(p, queries, r):
        span = slice(r * ROWS, (r + 1) * ROWS)
        lhs = jnp.concatenate([xr[p * CB + j, span, :] for j in range(CB)], axis=1)
        both = dot(lhs, queries, NT)
        for half in range(2):
            q = half * 128
            zacc[half, span] += jnp.where(even_row, both[:, q:q + 128], both[:, q + 256:q + 384])

    def products(p):
        ready(p)
        queries = weights(p)
        for r in range(2048 // ROWS):
            product(p, queries, r)

    def reduce_copy(step, r):
        src, dst = ((sb1, rb1), (sb2, rb2))[step]
        return pltpu.make_async_remote_copy(
            src_ref=src.at[r], dst_ref=dst.at[r],
            send_sem=rs_send.at[step, r], recv_sem=rs_recv.at[step, r],
            device_id=(x1, x3)[step ^ (r % 2)], device_id_type=MESH,
        )

    mates = (lay1, 3 - lay)

    def target(which, r):
        return part[pl.ds(pl.multiple_of(which * 64, 64), 64), r * 256:(r + 1) * 256]

    def scatter1(r):
        for half in range(2):
            both = zacc[half, pl.ds(r * ROWS, 256, 2), :] + zacc[half, pl.ds(r * ROWS + 1, 256, 2), :]
            part[half * 128:(half + 1) * 128, r * 256:(r + 1) * 256] = both.T
        sb1[r, 0] = target(mates[r % 2], r).astype(BF16)
        sb1[r, 1] = target(lay2, r).astype(BF16)
        reduce_copy(0, r).start()

    def scatter2(r):
        reduce_copy(0, r).wait_recv()
        sb2[r] = (target(mates[1 - r % 2], r) + rb1[r, 1].astype(F32)).astype(BF16)
        reduce_copy(1, r).start()

    def finish(r):
        reduce_copy(1, r).wait_recv()
        cols = slice(r * 256, (r + 1) * 256)
        total = target(lay, r) + rb1[r, 0].astype(F32) + rb2[r].astype(F32)
        out[:, cols] = jnp.where(ids == tids[:, cols], 0.0, total)

    def when(p, top, what):
        pl.when(jnp.logical_and(p >= 0, p < top))(functools.partial(what, p))

    for p in range(PARTS):
        for cb in range(p * CB, (p + 1) * CB):
            g[core, b, a, :, cb * 128:(cb + 1) * 128] = whole[pl.ds(cb, 16, 32), :].astype(BF16)
        go(p, "S1p", "S1m", "S1d")

    @pl.loop(0, PARTS + 8 - 1)
    def _(s):
        when(s, PARTS, step2)
        when(s - 4, PARTS, step3)
        when(s - 7, PARTS, step4)
        when(s - 8, PARTS - 1, products)

    place = lax.broadcasted_iota(jnp.int32, (64, 64), 0) == lax.broadcasted_iota(jnp.int32, (64, 64), 1)
    ids = jnp.sum(jnp.where(place, qids[...].astype(F32), 0.0), axis=1, keepdims=True).astype(jnp.int32)
    last = PARTS - 1
    ready(last)
    queries = weights(last)
    for r in range(4):
        product(last, queries, r)
        scatter1(r)
    for r in range(4):
        scatter2(r)
    for r in range(4):
        finish(r)

    for name in OPS:
        copy(name, 0, every).wait_send()

    for step in range(2):
        for r in range(4):
            reduce_copy(step, r).wait_send()


def body(train_grads, query_grads, basis_out, basis_in, eigenvalues, train_ids, query_ids):
    train = train_grads.reshape(1024, 2, 32, 128).transpose(0, 2, 1, 3)
    query = query_grads.reshape(8, 2, 32, 128).transpose(0, 2, 1, 3)
    vmem = pl.BlockSpec(memory_space=pltpu.VMEM)
    hbm = pl.BlockSpec(memory_space=pltpu.HBM)
    dma = pltpu.SemaphoreType.DMA
    scores = pl.pallas_call(
        kernel,
        out_shape=jax.ShapeDtypeStruct((64, 1024), F32),
        in_specs=[hbm] * 7,
        out_specs=vmem,
        scratch_shapes=[
            pltpu.VMEM((8, 32, 2, 128), BF16),
            pltpu.VMEM((2, 64, 64), F32),
            pltpu.VMEM((2, 64, 64), F32),
            pltpu.VMEM((2, 64, 64), F32),
            pltpu.VMEM((1, 1024), jnp.int32),
            pltpu.VMEM((1, 64), jnp.int32),
            pltpu.VMEM((32, 1024, 2, 128), BF16),
            pltpu.VMEM((512, 128), F32),
            pltpu.VMEM((2, 2, 128, 128), F32),
            pltpu.VMEM((512, 128), F32),
            pltpu.VMEM((256, 128), F32),
            pltpu.VMEM((2, 4, 4, 16, 4096), BF16),
            pltpu.VMEM((2, 2048, 128), F32),
            pltpu.VMEM((256, 1024), F32),
            pltpu.VMEM((4, 2, 64, 256), BF16),
            pltpu.VMEM((4, 2, 64, 256), BF16),
            pltpu.VMEM((4, 64, 256), BF16),
            pltpu.VMEM((4, 64, 256), BF16),
            dma((6,)),
            dma((32,)),
            dma((2,)),
            dma((len(OPS),)),
            dma((len(OPS), PARTS)),
            dma((2, 4)),
            dma((2, 4)),
        ],
        compiler_params=pltpu.CompilerParams(
            collective_id=0, has_side_effects=True, vmem_limit_bytes=50 * 2**20
        ),
    )(
        *(
            pltpu.with_memory_space_constraint(value, pltpu.HBM)
            for value in (
                train, query, basis_out, basis_in, eigenvalues,
                train_ids.reshape(1, -1), query_ids.reshape(1, -1),
            )
        )
    )
    return scores.T


def solution(mesh):
    placed = (
        P("rows", "layer", None),
        P("rows", "layer", None),
        P("layer", None, None),
        P("layer", None, None),
        P("layer", None, None),
        P("rows"),
        P("layer"),
    )
    return jax.shard_map(
        body, mesh=mesh, in_specs=placed, out_specs=P("rows", "layer"), check_vma=False
    )
```
